128 devices in a mesh: wide: 16 (over z, y), narrow: 8 (over x, core).
Axes of the slice: x: 4, y: 4, z: 4, core: 2. Of those that a mesh axis runs over, the one named last changes fastest.
Arguments:
- text_tokens: bfloat16 [16, 256, 3072], P('wide', 'narrow'), may hold values from -6 to 6
- image_tokens: bfloat16 [16, 512, 3072], P('wide', 'narrow'), may hold values from -6 to 6
- extra_tokens: bfloat16 [16, 128, 3072], P('wide', 'narrow'), may hold values from -6 to 6
- text_pos: int32 [3, 16, 256], P(None, 'wide'), may hold values from 0 to 63
- image_pos: int32 [3, 16, 512], P(None, 'wide'), may hold values from 0 to 63
- extra_pos: int32 [3, 16, 128], P(None, 'wide'), may hold values from 0 to 63
- extra_counts: int32 [128], replicated, may hold values from 1 to 16, 896 in all
- request_group: int32 [16], replicated, may hold values from 0 to 15, each once
- step_index: int32 [17], replicated, may hold values from 0 to 3
- mod_table: float32 [4, 3, 3072], replicated, may hold values from -3 to 3
- final_table: float32 [4, 2, 3072], replicated, may hold values from -3 to 3
- qkv_weight: bfloat16 [3, 3072, 3072], P(None, None, 'narrow'), may hold values from -0.109375 to 0.109375
- q_scale: float32 [128], replicated, may hold values from 1 to 2.5
- k_scale: float32 [128], replicated, may hold values from 1 to 2.5
- attn_out_weight: bfloat16 [3072, 3072], P('narrow'), may hold values from -0.046875 to 0.046875
- mlp_in_weight: bfloat16 [3072, 12288], P('wide', 'narrow'), may hold values from -0.109375 to 0.109375
- mlp_out_weight: bfloat16 [12288, 3072], P('narrow', 'wide'), may hold values from -0.046875 to 0.046875
- proj_weight: bfloat16 [3072, 64], replicated, may hold values from -0.109375 to 0.109375
- stencil: float32 [9, 64], replicated, may hold values from -2 to 2
- latent: float32 [16, 16, 2048], P('wide', 'narrow'), may hold values from -6 to 6
Outputs:
- text_out: bfloat16 [16, 256, 3072], P('wide', 'narrow')
- image_out: bfloat16 [16, 512, 3072], P('wide', 'narrow')
- extra_out: bfloat16 [16, 128, 3072], P('wide', 'narrow')
- latent_next: float32 [16, 16, 2048], P('wide', 'narrow')
The draws below stay inside these ranges and needn't reach their ends.
Inputs may be any that keep to these rules, and one draw needn't show every extreme that they name: extra_counts[d] live slots of the split request on device d (devices ordered along wide, then narrow); they sum to 896, and some device holds exactly 16. `request_group`: a permutation of the requests.
All inputs are finite; a program needn't handle non-finite values.
Results may differ from the reference program's by a relative error of at most 0.01.
Values may be sent and summed in bfloat16 or wider, within the bound.
No kernel may reach another device: no remote copies, remote signals or barrier semaphores. Data moves between devices by JAX's collectives and lax.ppermute only.
A program may use at most 128 MiB of HBM per device.

```python
import math
import jax
import jax.numpy as jnp
import numpy as np
from jax import lax

D = 3072
HD = 128
FF = 12288
C = 64
TXT = 256
IMG_H = 16
IMG_W = 32
STEPS = 4
XCAP = 16
GROUPS = 16
IMG = 512
EG = 128
X_LEN = 896
N_NARROW = 8
DEVICES = 128


def with_ends(values, rng, smallest, largest):
    place = [jax.random.randint(jax.random.fold_in(rng, axis), (), 0, length) for axis, length in enumerate(values.shape)]
    widest = values.shape.index(max(values.shape))
    neighbour = place[:widest] + [(place[widest] + 1) % values.shape[widest]] + place[widest + 1:]
    return values.at[tuple(place)].set(smallest).at[tuple(neighbour)].set(largest)


def shard_levels(stream_key, shape, cuts, low, top_value):
    def one(axis_at, blocks):
        heights = jax.random.uniform(jax.random.fold_in(jax.random.fold_in(stream_key, 6), axis_at), (blocks,), jnp.float32, low / len(cuts), top_value / len(cuts))
        return jnp.repeat(jnp.exp(heights), shape[axis_at] // blocks).reshape((-1,) + (1,) * (len(shape) - axis_at - 1))

    level = one(*cuts[0])
    for cut in cuts[1:]:
        level = level * one(*cut)
    return level


def split_up(count, total, limit, lean):
    weights = [(1 << 20) // math.isqrt(rank ** lean) + 1 for rank in range(2, count + 1)]
    spare, counts = total - limit - (count - 1), [1] * (count - 1)
    while spare > 0:
        candidates = [i for i in range(count - 1) if counts[i] < limit]
        whole, left = sum([weights[i] for i in candidates]), spare
        for i in candidates:
            more = min(limit - counts[i], max(1, left * weights[i] // whole), spare)
            counts[i] = counts[i] + more
            spare = spare - more
    return np.array([limit] + counts)


def uneven(stream_key, number_of, total, reach, lean):
    if number_of == 2:
        one = jax.random.randint(stream_key, (), max(1, total - reach), min(reach, total - 1) + 1)
        return jnp.stack([one, total - one])
    lengths = jnp.asarray(split_up(number_of, total, reach, lean), jnp.int32)
    pairs = (number_of - 1) // 2
    donor, sink = lengths[1:1 + 2 * pairs:2], lengths[2:2 + 2 * pairs:2]
    slack = jnp.minimum(donor - 1, reach - sink)
    shifted = jax.random.randint(jax.random.fold_in(stream_key, 1), (pairs,), 0, 1 << 20) % (slack + 1)
    lengths = lengths.at[1:1 + 2 * pairs:2].set(donor - shifted).at[2:2 + 2 * pairs:2].set(sink + shifted)
    return lengths[jax.random.permutation(jax.random.fold_in(stream_key, 2), number_of)]


def gaussian(rng, shape, width, most, cuts=(), kind=jnp.bfloat16):
    values = jax.random.normal(rng, shape, jnp.float32) * width
    if len(cuts) > 0:
        values = shard_levels(rng, shape, cuts, -0.22, 0.18) * values
    return jnp.clip(values, min=-most, max=most).astype(kind)


def setup_inputs(seed: int = 0) -> dict:
    key_of = jax.random.split(jax.random.key(seed), 21)
    text_tokens = gaussian(key_of[0], (GROUPS, TXT, D), 1.0, 6.0, ((0, 16), (1, 8)))
    image_tokens = gaussian(key_of[1], (GROUPS, IMG, D), 1.0, 6.0, ((0, 16), (1, 8)))
    extra_tokens = gaussian(key_of[2], (GROUPS, EG, D), 1.0, 6.0, ((0, 16), (1, 8)))
    text_pos = with_ends(jax.random.randint(key_of[3], (3, GROUPS, TXT), 0, 64), jax.random.fold_in(key_of[3], 1), 0, 63).astype(jnp.int32)
    image_pos = with_ends(jax.random.randint(key_of[4], (3, GROUPS, IMG), 0, 64), jax.random.fold_in(key_of[4], 1), 0, 63).astype(jnp.int32)
    extra_pos = with_ends(jax.random.randint(key_of[5], (3, GROUPS, EG), 0, 64), jax.random.fold_in(key_of[5], 1), 0, 63).astype(jnp.int32)
    extra_counts = uneven(key_of[6], DEVICES, X_LEN, XCAP, 2).astype(jnp.int32)
    request_group = jax.random.permutation(key_of[7], GROUPS).astype(jnp.int32)
    step_index = with_ends(jax.random.randint(key_of[8], (GROUPS + 1,), 0, STEPS), jax.random.fold_in(key_of[8], 1), 0, STEPS - 1).astype(jnp.int32)
    mod_table = gaussian(key_of[9], (STEPS, 3, D), 0.5, 3.0, (), jnp.float32)
    final_table = gaussian(key_of[10], (STEPS, 2, D), 0.5, 3.0, (), jnp.float32)
    qkv_weight = gaussian(key_of[11], (3, D, D), D ** -0.5, 0.109375, ((2, 8),))
    q_scale = jnp.clip(jnp.exp(jax.random.uniform(key_of[12], (HD,), jnp.float32, math.log(1.0), math.log(2.5))), 1.0, 2.5)
    k_scale = jnp.clip(jnp.exp(jax.random.uniform(key_of[13], (HD,), jnp.float32, math.log(1.0), math.log(2.5))), 1.0, 2.5)
    attn_out_weight = gaussian(key_of[14], (D, D), (D + FF) ** -0.5, 0.046875, ((0, 8),))
    mlp_in_weight = gaussian(key_of[15], (D, FF), D ** -0.5, 0.109375, ((0, 16), (1, 8)))
    mlp_out_weight = gaussian(key_of[16], (FF, D), (D + FF) ** -0.5, 0.046875, ((0, 8), (1, 16)))
    proj_weight = gaussian(key_of[17], (D, C), D ** -0.5, 0.109375)
    stencil = gaussian(key_of[18], (9, C), 0.4, 2.0, (), jnp.float32)
    latent = gaussian(key_of[19], (GROUPS, IMG_H, IMG_W * C), 1.0, 6.0, ((0, 16), (1, 8)), jnp.float32)
    return {"text_tokens": text_tokens, "image_tokens": image_tokens, "extra_tokens": extra_tokens, "text_pos": text_pos, "image_pos": image_pos, "extra_pos": extra_pos, "extra_counts": extra_counts, "request_group": request_group, "step_index": step_index, "mod_table": mod_table, "final_table": final_table, "qkv_weight": qkv_weight, "q_scale": q_scale, "k_scale": k_scale, "attn_out_weight": attn_out_weight, "mlp_in_weight": mlp_in_weight, "mlp_out_weight": mlp_out_weight, "proj_weight": proj_weight, "stencil": stencil, "latent": latent}


EPSILON = 1e-06
ROPE_BASE = 10000.0

def layer_norm(values):
    centre = lax.optimization_barrier(jnp.mean(values, axis=-1, keepdims=True))
    centred = values - centre
    spread = lax.optimization_barrier(jnp.mean(centred * centred, axis=-1, keepdims=True))
    return centred * lax.rsqrt(spread + EPSILON)

def modulate(tokens, shift_vec, scale_vec):
    return layer_norm(tokens.astype(jnp.float32)) * (1.0 + scale_vec) + shift_vec

def section_widths(head_dim):
    return (head_dim // 8, 7 * head_dim // 16, 7 * head_dim // 16)

def rope_tables(positions, head_dim):
    angle_list = []
    for axis_id, section in enumerate(section_widths(head_dim)):
        half_width = section // 2
        exponent = -2.0 * jnp.arange(half_width, dtype=jnp.float32) / section
        frequency = jnp.power(jnp.float32(ROPE_BASE), exponent)
        angles = positions[axis_id].astype(jnp.float32)[:, None] * frequency[None, :]
        angle_list.append(angles)
        angle_list.append(angles)
    angles = jnp.concatenate(angle_list, axis=1)
    return (jnp.cos(angles), jnp.sin(angles))

def rotate(head_rows, cosine, sine_vals):
    pieces = []
    offset = 0
    for section in section_widths(head_rows.shape[-1]):
        half_width = section // 2
        first_half = head_rows[..., offset:offset + half_width]
        second = head_rows[..., offset + half_width:offset + section]
        pieces.append(-second)
        pieces.append(first_half)
        offset += section
    partner = jnp.concatenate(pieces, axis=-1)
    return head_rows * cosine[:, None, :] + partner * sine_vals[:, None, :]

def head_norm(head_rows, gain_vec):
    square = lax.optimization_barrier(jnp.mean(head_rows * head_rows, axis=-1, keepdims=True))
    return head_rows * lax.rsqrt(square + EPSILON) * gain_vec

def project_heads(modulated, qkv_parts, q_scale, k_scale, positions):
    head_dim = q_scale.shape[0]
    row_total = modulated.shape[0]
    cosine, sine_vals = rope_tables(positions, head_dim)
    outputs = []
    for which in range(3):
        projected = jnp.dot(modulated, qkv_parts[which], preferred_element_type=jnp.float32)
        projected = projected.reshape(row_total, -1, head_dim)
        if which == 0:
            projected = rotate(head_norm(projected, q_scale), cosine, sine_vals)
        if which == 1:
            projected = rotate(head_norm(projected, k_scale), cosine, sine_vals)
        outputs.append(projected.astype(jnp.bfloat16))
    return outputs

def attend(queries, key_rows, value_rows, live_mask):
    factor = 1.0 / math.sqrt(queries.shape[-1])
    query_heads = jnp.transpose(queries, (1, 0, 2))
    key_heads = jnp.transpose(key_rows, (1, 0, 2))
    value_heads = jnp.transpose(value_rows, (1, 0, 2))

    def per_head(head_items):
        query_h, key_h, value_h = head_items
        scores = jnp.dot(query_h, key_h.T, preferred_element_type=jnp.float32) * factor
        weights = jnp.exp(scores)
        if live_mask is not None:
            weights = jnp.where(live_mask[None, :], weights, 0.0)
        running = lax.optimization_barrier(jnp.sum(weights, axis=1))
        accumulated = jnp.dot(weights.astype(jnp.bfloat16), value_h, preferred_element_type=jnp.float32)
        return (accumulated, running)
    return lax.map(per_head, (query_heads, key_heads, value_heads))

def finish(accumulated, running):
    normed = accumulated / running[..., None]
    normed = jnp.transpose(normed, (1, 0, 2))
    return normed.reshape(normed.shape[0], -1).astype(jnp.bfloat16)

def narrow_partials(attn_rows, mlp_act, attn_out_weight, mlp_out_weight, shards):
    attn_cols = attn_rows.shape[1] // shards
    mlp_cols = mlp_act.shape[1] // shards

    def one_shard(shard_id):
        attn_part = lax.dynamic_slice_in_dim(attn_rows, shard_id * attn_cols, attn_cols, 1)
        attn_rows_w = lax.dynamic_slice_in_dim(attn_out_weight, shard_id * attn_cols, attn_cols, 0)
        mlp_part = lax.dynamic_slice_in_dim(mlp_act, shard_id * mlp_cols, mlp_cols, 1)
        mlp_rows_w = lax.dynamic_slice_in_dim(mlp_out_weight, shard_id * mlp_cols, mlp_cols, 0)
        partial_value = jnp.dot(attn_part, attn_rows_w, preferred_element_type=jnp.float32) + jnp.dot(mlp_part, mlp_rows_w, preferred_element_type=jnp.float32)
        rounded = lax.optimization_barrier(partial_value.astype(jnp.bfloat16))
        return rounded.astype(jnp.float32)
    return lax.optimization_barrier(jnp.sum(lax.map(one_shard, jnp.arange(shards, dtype=jnp.int32)), axis=0))

def noise_level(step_value):
    level = 1.0 - step_value.astype(jnp.float32) / STEPS
    return 3.0 * level / (1.0 + 2.0 * level)

def final_velocity(hidden_rows, final_mod, proj_weight):
    normed = modulate(hidden_rows, final_mod[0], final_mod[1]).astype(jnp.bfloat16)
    return jnp.dot(normed, proj_weight, preferred_element_type=jnp.float32)

def smooth(padded_rows, stencil, grid_width):
    channels = stencil.shape[1]
    row_total = padded_rows.shape[0] - 2
    cells = padded_rows.reshape(row_total + 2, grid_width, channels)
    cells = jnp.pad(cells, ((0, 0), (1, 1), (0, 0)))
    result = jnp.zeros((row_total, grid_width, channels), jnp.float32)
    for row_tap in range(3):
        for col_tap in range(3):
            result = result + stencil[3 * row_tap + col_tap] * cells[row_tap:row_tap + row_total, col_tap:col_tap + grid_width]
    return result.reshape(row_total, grid_width * channels)

def run_block(tokens, modulation, positions, live_mask, qkv_weight, q_scale, k_scale, attn_out_weight, mlp_in_weight, mlp_out_weight):
    modulated = modulate(tokens, modulation[0], modulation[1]).astype(jnp.bfloat16)
    queries, key_rows, value_rows = project_heads(modulated, qkv_weight, q_scale, k_scale, positions)
    accumulated, running = attend(queries, key_rows, value_rows, live_mask)
    attn_rows = finish(accumulated, running)
    mlp_act = jax.nn.gelu(jnp.dot(modulated, mlp_in_weight, preferred_element_type=jnp.float32), approximate=True).astype(jnp.bfloat16)
    summed = narrow_partials(attn_rows, mlp_act, attn_out_weight, mlp_out_weight, N_NARROW)
    return tokens.astype(jnp.float32) + modulation[2] * summed

def reference(text_tokens, image_tokens, extra_tokens, text_pos, image_pos, extra_pos, extra_counts, request_group, step_index, mod_table, final_table, qkv_weight, q_scale, k_scale, attn_out_weight, mlp_in_weight, mlp_out_weight, proj_weight, stencil, latent):
    group_steps = step_index[request_group]
    extra_step_value = step_index[request_group.shape[0]]
    channels = proj_weight.shape[1]
    grid_width = latent.shape[2] // channels
    text_count = text_tokens.shape[1]

    def one_request(items):
        text_rows, image_rows, text_place, image_place, step_here, latent_rows = items
        tokens = jnp.concatenate([text_rows, image_rows], axis=0)
        positions = jnp.concatenate([text_place, image_place], axis=1)
        hidden = run_block(tokens, mod_table[step_here], positions, None, qkv_weight, q_scale, k_scale, attn_out_weight, mlp_in_weight, mlp_out_weight)
        velocity = final_velocity(hidden[text_count:], final_table[step_here], proj_weight)
        padded = jnp.pad(velocity.reshape(-1, grid_width * channels), ((1, 1), (0, 0)))
        time_delta = noise_level(step_here + 1) - noise_level(step_here)
        latent_next = latent_rows + time_delta * smooth(padded, stencil, grid_width)
        rounded = hidden.astype(jnp.bfloat16)
        return (rounded[:text_count], rounded[text_count:], latent_next)
    text_out, image_out, latent_next = lax.map(one_request, (text_tokens, image_tokens, jnp.transpose(text_pos, (1, 0, 2)), jnp.transpose(image_pos, (1, 0, 2)), group_steps, latent))
    slot_total = extra_tokens.shape[0] * extra_tokens.shape[1]
    slot_cap = slot_total // extra_counts.shape[0]
    extra_rows = extra_tokens.reshape(slot_total, extra_tokens.shape[2])
    slot_ids = jnp.arange(slot_total, dtype=jnp.int32)
    live_mask = slot_ids % slot_cap < extra_counts[slot_ids // slot_cap]
    positions = extra_pos.reshape(3, slot_total)
    hidden = run_block(extra_rows, mod_table[extra_step_value], positions, live_mask, qkv_weight, q_scale, k_scale, attn_out_weight, mlp_in_weight, mlp_out_weight)
    extra_out = jnp.where(live_mask[:, None], hidden, 0.0).astype(jnp.bfloat16).reshape(extra_tokens.shape)
    return (text_out, image_out, extra_out, latent_next)
```

```python
import functools
import math

import jax
import jax.numpy as jnp
from jax import lax
from jax.experimental import pallas as pl
from jax.experimental.pallas import tpu as pltpu
from jax.sharding import PartitionSpec as P

STEPS = 4
EPSILON = 1e-06
ROPE_BASE = 10000.0
MIB = 1 << 20
F32 = jnp.float32
BF16 = jnp.bfloat16
NT = (((1,), (1,)), ((), ()))

VMEM = pl.BlockSpec(memory_space=pltpu.VMEM)
SMEM = pl.BlockSpec(memory_space=pltpu.SMEM)
ANY = pl.BlockSpec(memory_space=pl.ANY)


def section_widths(head_dim):
    return (head_dim // 8, 7 * head_dim // 16, 7 * head_dim // 16)


def layer_norm(values):
    centre = jnp.mean(values, axis=-1, keepdims=True)
    centred = values - centre
    spread = jnp.mean(centred * centred, axis=-1, keepdims=True)
    return centred * lax.rsqrt(spread + EPSILON)


def cost(flops, moved, exps=0):
    return pl.CostEstimate(flops=int(flops), bytes_accessed=int(moved), transcendentals=int(exps))


def wide_shift(dz, dy):
    return [(z * 4 + y, ((z + dz) % 4) * 4 + (y + dy) % 4) for z in range(4) for y in range(4)]


def chip_shift(step):
    return [(x * 2 + c, ((x + step) % 4) * 2 + c) for x in range(4) for c in range(2)]


CORE_SWAP = [(i, i ^ 1) for i in range(8)]
RING_ORDER = (0, -1, 1, 2)


def ring(block, shift, first, last):
    before = lax.ppermute(block, "wide", shift(1))
    after = lax.ppermute(block, "wide", shift(-1))
    far_first = lax.ppermute(first(before), "wide", shift(1))
    far_last = lax.ppermute(last(after), "wide", shift(-1))
    return before, after, far_first, far_last


def along_y(step):
    return wide_shift(0, step)


def along_z(step):
    return wide_shift(step, 0)


def collect(block, shift_one, shift_two):
    half = block.shape[0] // 2
    before, after, far_first, far_last = ring(
        block, shift_one, lambda b: b[:half], lambda b: b[half:]
    )
    quad = jnp.concatenate([block, before, after, far_first, far_last], axis=0)
    two = 2 * block.shape[0]
    return (quad,) + ring(quad, shift_two, lambda b: b[:two], lambda b: b[two:])


def gather_rows(own):
    half = own.shape[0] // 2
    swap = functools.partial(lax.ppermute, axis_name="narrow", perm=CORE_SWAP)
    nxt = lax.ppermute(own, "narrow", chip_shift(-1))
    prv = lax.ppermute(own, "narrow", chip_shift(1))
    far_a = lax.ppermute(nxt[:half], "narrow", chip_shift(-1))
    far_b = lax.ppermute(prv[half:], "narrow", chip_shift(1))
    return jnp.concatenate(
        [own, nxt, far_a, far_b, prv, swap(own), swap(nxt), swap(far_a), swap(far_b), swap(prv)], axis=0
    )


def scatter_sum(partial):
    rows, columns = partial.shape[0] // 8, partial.shape[1]
    half = columns // 2
    other = lax.ppermute(partial[4 * rows :], "narrow", CORE_SWAP).astype(F32)
    pair = partial[: 4 * rows].astype(F32) + other
    far = pair[2 * rows : 3 * rows].astype(BF16)
    from_prv = lax.ppermute(far[:, :half], "narrow", chip_shift(1)).astype(F32)
    from_nxt = lax.ppermute(far[:, half:], "narrow", chip_shift(-1)).astype(F32)
    to_nxt = pair[rows : 2 * rows]
    to_prv = pair[3 * rows :]
    to_nxt = jnp.concatenate([to_nxt[:, :half] + from_prv, to_nxt[:, half:]], axis=1).astype(BF16)
    to_prv = jnp.concatenate([to_prv[:, :half], to_prv[:, half:] + from_nxt], axis=1).astype(BF16)
    one = lax.ppermute(to_nxt, "narrow", chip_shift(1))
    two = lax.ppermute(to_prv, "narrow", chip_shift(-1))
    return pair[:rows], one, two


def modulate_kernel(steps, text, image, extra, mod_table, out):
    here, there = steps[0], steps[1]
    shift, scale = mod_table[here, 0:1, :], mod_table[here, 1:2, :]
    row = 0
    for ref in (text, image):
        rows = ref.shape[0]
        out[row : row + rows, :] = (layer_norm(ref[...].astype(F32)) * (1.0 + scale) + shift).astype(BF16)
        row += rows
    shift, scale = mod_table[there, 0:1, :], mod_table[there, 1:2, :]
    rows = extra.shape[0]
    out[row : row + rows, :] = (layer_norm(extra[...].astype(F32)) * (1.0 + scale) + shift).astype(BF16)


def modulate(steps, text, image, extra, mod_table):
    rows = text.shape[0] + image.shape[0] + extra.shape[0]
    return pl.pallas_call(
        modulate_kernel,
        out_shape=jax.ShapeDtypeStruct((rows, text.shape[1]), BF16),
        in_specs=[SMEM, VMEM, VMEM, VMEM, VMEM],
        out_specs=VMEM,
        compiler_params=pltpu.CompilerParams(vmem_limit_bytes=8 * MIB),
        cost_estimate=cost(1e6, 2 * MIB),
    )(steps, text, image, extra, mod_table)


def partner_of(values):
    lane = lax.broadcasted_iota(jnp.int32, values.shape, 1)
    width = values.shape[1]
    result = None
    offset = 0
    rolled = {}
    for section in section_widths(width):
        half = section // 2
        for amount, start in ((width - half, offset), (half, offset + half)):
            if amount not in rolled:
                rolled[amount] = pltpu.roll(values, amount, 1)
            result = rolled[amount] if result is None else jnp.where(lane >= start, rolled[amount], result)
        offset += section
    return result


def heads_kernel(blocks, own, x, weight, gains, cosine, sine, request, extra):
    which = pl.program_id(0)
    total = x.shape[0]
    rows = total // blocks
    taken = rows - own
    step = 2 * rows
    heads = weight.shape[2] // 128

    def tile(index, carry):
        start = pl.multiple_of(index * step, 32)
        acc = jnp.dot(x[pl.ds(start, step), :], weight[0], preferred_element_type=F32)

        def put(head, values):
            for part in range(2):
                first = part * rows
                block = 2 * index + part
                request[0, head, pl.ds(pl.multiple_of(block * taken, 32), taken), :] = values[first : first + taken]
                extra[0, head, pl.ds(pl.multiple_of(block * own, 16), own), :] = values[first + taken : first + rows]

        @pl.when(which < 2)
        def _():
            gain = gains[pl.ds(which, 1), :]
            cos = cosine[pl.ds(start, step), :]
            sin = sine[pl.ds(start, step), :]
            for head in range(heads):
                part = acc[:, head * 128 : (head + 1) * 128]
                square = jnp.mean(part * part, axis=1, keepdims=True)
                part = part * lax.rsqrt(square + EPSILON) * gain
                put(head, (part * cos + partner_of(part) * sin).astype(BF16))

        @pl.when(which == 2)
        def _():
            for head in range(heads):
                put(head, acc[:, head * 128 : (head + 1) * 128].astype(BF16))

        return carry

    lax.fori_loop(0, total // step, tile, 0)


def project_heads(x, weight, gains, cosine, sine, blocks, own):
    total, width = x.shape
    heads = weight.shape[2] // 128
    extra = blocks * own
    request = total - extra
    return pl.pallas_call(
        functools.partial(heads_kernel, blocks, own),
        grid=(3,),
        out_shape=(
            jax.ShapeDtypeStruct((3, heads, request, 128), BF16),
            jax.ShapeDtypeStruct((3, heads, extra, 128), BF16),
        ),
        in_specs=[
            VMEM,
            pl.BlockSpec((1, width, weight.shape[2]), lambda i: (i, 0, 0)),
            VMEM,
            VMEM,
            VMEM,
        ],
        out_specs=(
            pl.BlockSpec((1, heads, request, 128), lambda i: (i, 0, 0, 0)),
            pl.BlockSpec((1, heads, extra, 128), lambda i: (i, 0, 0, 0)),
        ),
        compiler_params=pltpu.CompilerParams(vmem_limit_bytes=28 * MIB),
        cost_estimate=cost(6 * total * width * weight.shape[2], 16 * MIB),
    )(x, weight, gains, cosine, sine)


def weigh(query, keys, values, live):
    scores = lax.dot_general(query, keys, NT, preferred_element_type=F32)
    weights = jnp.exp(scores * (1.0 / math.sqrt(query.shape[1])))
    if live is not None:
        weights = jnp.where(live, weights, 0.0)
    running = jnp.sum(weights, axis=1, keepdims=True)
    total = jnp.dot(weights.astype(BF16), values, preferred_element_type=F32)
    return (total / running).astype(BF16)


def request_kernel(query, keys, values, out):
    step = 256
    for start in range(0, query.shape[2], step):
        out[start : start + step, :] = weigh(query[0, 0, start : start + step, :], keys[0, 0], values[0, 0], None)


def attend_request(heads):
    count, rows = heads.shape[1], heads.shape[2]

    def block(which):
        return pl.BlockSpec((1, 1, rows, 128), lambda h: (which, h, 0, 0))

    return pl.pallas_call(
        request_kernel,
        grid=(count,),
        out_shape=jax.ShapeDtypeStruct((rows, count * 128), BF16),
        in_specs=[block(0), block(1), block(2)],
        out_specs=pl.BlockSpec((rows, 128), lambda h: (0, h)),
        compiler_params=pltpu.CompilerParams(vmem_limit_bytes=16 * MIB),
        cost_estimate=cost(4 * count * rows * rows * 128, 5 * MIB, count * rows * rows),
    )(heads, heads, heads)


def extra_kernel(blocks, query, live, done, *refs):
    keys, values, out = refs[:5], refs[5:10], refs[10]
    every_key = jnp.concatenate([ref[i, 0] for ref in keys for i in range(ref.shape[0])], axis=0)
    every_value = jnp.concatenate([ref[i, 0] for ref in values for i in range(ref.shape[0])], axis=0)
    attended = weigh(query[0, 0], every_key, every_value, live[...] > 0)
    taken, own = done.shape[0] // blocks, attended.shape[0] // blocks
    rows = taken + own
    for block in range(blocks):
        out[block * rows : block * rows + taken, :] = done[block * taken : (block + 1) * taken, :]
        out[block * rows + taken : (block + 1) * rows, :] = attended[block * own : (block + 1) * own, :]


def attend_extra(heads, live, done, pieces, blocks):
    count, rows = heads.shape[1], heads.shape[2]

    def pair(first):
        return [
            pl.BlockSpec((piece.shape[0], 1, rows, 128), lambda h: (0, first + h, 0, 0)) for piece in pieces
        ]

    total = done.shape[0] + rows
    return pl.pallas_call(
        functools.partial(extra_kernel, blocks),
        grid=(count,),
        out_shape=jax.ShapeDtypeStruct((total, count * 128), BF16),
        in_specs=[
            pl.BlockSpec((1, 1, rows, 128), lambda h: (0, h, 0, 0)),
            pl.BlockSpec(live.shape, lambda h: (0, 0)),
            pl.BlockSpec((done.shape[0], 128), lambda h: (0, h)),
        ]
        + pair(0)
        + pair(count),
        out_specs=pl.BlockSpec((total, 128), lambda h: (0, h)),
        compiler_params=pltpu.CompilerParams(vmem_limit_bytes=16 * MIB),
        cost_estimate=cost(4 * count * rows * live.shape[1] * 128, 5 * MIB, count * rows * live.shape[1]),
    )(heads, live, done, *pieces, *pieces)


def gelu(values):
    inner = math.sqrt(2.0 / math.pi) * (values + 0.044715 * (values * values * values))
    return values * (0.5 * (1.0 + jnp.tanh(inner)))


def hidden_kernel(place, x, *refs):
    pieces, out, weight, done = refs[:10], refs[10], refs[11], refs[12]
    z, y = place[0], place[1]
    half = weight.shape[0] // 32
    copies = []

    def fetch(ref, index, dz, dy, part):
        group = lax.rem(z + dz + 4, 4) * 4 + lax.rem(y + dy + 4, 4)
        start = pl.multiple_of(group * (2 * half) + part * half, 32)
        copy = pltpu.make_async_copy(
            ref.at[pl.ds(index * half, half), :], weight.at[pl.ds(start, half), :], done.at[len(copies)]
        )
        copy.start()
        copies.append(copy)

    for part in range(2):
        quad, before, after, far_first, far_last = pieces[5 * part : 5 * part + 5]
        for outer, ref, span, base in (
            (0, quad, range(4), 0),
            (-1, before, range(4), 0),
            (1, after, range(4), 0),
            (2, far_first, range(2), 0),
            (2, far_last, range(2, 4), 2),
        ):
            for index in span:
                inner = RING_ORDER[index]
                dz, dy = (outer, inner) if part == 0 else (inner, outer)
                fetch(ref, index - base, dz, dy, part)
    for copy in copies:
        copy.wait()
    step = 256

    def tile(index, carry):
        columns = pl.ds(pl.multiple_of(index * step, step), step)
        acc = jnp.dot(x[...], weight[:, columns], preferred_element_type=F32)
        out[:, columns] = gelu(acc).astype(BF16)
        return carry

    lax.fori_loop(0, out.shape[1] // step, tile, 0)


def hidden_units(place, x, pieces):
    rows, width = x.shape
    units = pieces[0].shape[1]
    return pl.pallas_call(
        hidden_kernel,
        out_shape=jax.ShapeDtypeStruct((rows, units), BF16),
        in_specs=[SMEM, VMEM] + [ANY] * 10,
        out_specs=VMEM,
        scratch_shapes=[pltpu.VMEM((width, units), BF16), pltpu.SemaphoreType.DMA((32,))],
        compiler_params=pltpu.CompilerParams(vmem_limit_bytes=26 * MIB),
        cost_estimate=cost(2 * rows * width * units, 18 * MIB, rows * units),
    )(place, x, *pieces)


def output_kernel(act, weight, attended, attn_weight, out):
    acc = lax.dot_general(act[...], weight[...], NT, preferred_element_type=F32)
    acc = acc + jnp.dot(attended[...], attn_weight[...], preferred_element_type=F32)
    out[...] = acc.astype(BF16)


def output_part(act, weight, attended, attn_weight, first, columns, step=256):
    rows, units = act.shape
    base = first // step
    return pl.pallas_call(
        output_kernel,
        grid=(columns // step,),
        out_shape=jax.ShapeDtypeStruct((rows, columns), BF16),
        in_specs=[
            pl.BlockSpec((rows, units), lambda i: (0, 0)),
            pl.BlockSpec((step, units), lambda i: (base + i, 0)),
            pl.BlockSpec((rows, attended.shape[1]), lambda i: (0, 0)),
            pl.BlockSpec((attn_weight.shape[0], step), lambda i: (0, base + i)),
        ],
        out_specs=pl.BlockSpec((rows, step), lambda i: (0, i)),
        compiler_params=pltpu.CompilerParams(vmem_limit_bytes=20 * MIB),
        cost_estimate=cost(2 * rows * columns * (units + attended.shape[1]), 8 * MIB),
    )(act, weight, attended, attn_weight)


def finish_kernel(chunks, scalars, text, image, extra, mod_table, final_table, proj, *refs):
    sums, (text_out, image_out, extra_out, velocity, hidden) = refs[: 3 * chunks], refs[3 * chunks :]
    here, there, count = scalars[0], scalars[1], scalars[2]
    width = text.shape[1] // chunks
    rows_text, rows_image = text.shape[0], image.shape[0]
    for chunk in range(chunks):
        own, one, two = sums[3 * chunk : 3 * chunk + 3]
        total = own[...] + one[...].astype(F32) + two[...].astype(F32)
        columns = slice(chunk * width, (chunk + 1) * width)
        gate = mod_table[here, 2:3, columns]
        text_out[:, columns] = (text[:, columns].astype(F32) + gate * total[:rows_text]).astype(BF16)
        states = image[:, columns].astype(F32) + gate * total[rows_text : rows_text + rows_image]
        hidden[:, columns] = states
        image_out[:, columns] = states.astype(BF16)
        gate = mod_table[there, 2:3, columns]
        slots = extra[:, columns].astype(F32) + gate * total[rows_text + rows_image :]
        live = lax.broadcasted_iota(jnp.int32, slots.shape, 0) < count
        extra_out[:, columns] = jnp.where(live, slots, 0.0).astype(BF16)
    shift, scale = final_table[here, 0:1, :], final_table[here, 1:2, :]
    normed = (layer_norm(hidden[...]) * (1.0 + scale) + shift).astype(BF16)
    velocity[...] = lax.dot_general(normed, proj[...], NT, preferred_element_type=F32)


def finish(scalars, text, image, extra, mod_table, final_table, proj, sums):
    width = text.shape[1]
    flat = [part for chunk in sums for part in chunk]
    return pl.pallas_call(
        functools.partial(finish_kernel, len(sums)),
        out_shape=(
            jax.ShapeDtypeStruct(text.shape, BF16),
            jax.ShapeDtypeStruct(image.shape, BF16),
            jax.ShapeDtypeStruct(extra.shape, BF16),
            jax.ShapeDtypeStruct((image.shape[0], proj.shape[0]), F32),
        ),
        in_specs=[SMEM] + [VMEM] * (6 + len(flat)),
        out_specs=(VMEM,) * 4,
        scratch_shapes=[pltpu.VMEM((image.shape[0], width), F32)],
        compiler_params=pltpu.CompilerParams(vmem_limit_bytes=16 * MIB),
        cost_estimate=cost(1e7, 5 * MIB),
    )(scalars, text, image, extra, mod_table, final_table, proj, *flat)


def smooth_kernel(columns, delta, above, middle, below, stencil, latent, out):
    rows = middle.shape[0]
    cells = jnp.concatenate([above[...], middle[...], below[...]], axis=0)
    column = lax.rem(lax.broadcasted_iota(jnp.int32, middle.shape, 0), columns)
    total = jnp.zeros(middle.shape, F32)
    for row_tap in range(3):
        band = cells[row_tap * columns : row_tap * columns + rows]
        for col_tap in range(3):
            moved = band if col_tap == 1 else pltpu.roll(band, (1 - col_tap) % rows, 0)
            place = column + (col_tap - 1)
            moved = jnp.where((place >= 0) & (place < columns), moved, 0.0)
            tap = 3 * row_tap + col_tap
            total = total + stencil[tap : tap + 1, :] * moved
    out[...] = latent[...] + delta[0] * total


def smooth(delta, above, middle, below, stencil, latent, columns):
    return pl.pallas_call(
        functools.partial(smooth_kernel, columns),
        out_shape=jax.ShapeDtypeStruct(middle.shape, F32),
        in_specs=[SMEM] + [VMEM] * 5,
        out_specs=VMEM,
        cost_estimate=cost(1e5, 1e5),
    )(delta, above, middle, below, stencil, latent)


def rope_tables(positions, head_dim):
    angle_list, signs = [], []
    for axis_id, section in enumerate(section_widths(head_dim)):
        half_width = section // 2
        exponent = -2.0 * jnp.arange(half_width, dtype=F32) / section
        frequency = jnp.power(F32(ROPE_BASE), exponent)
        angles = positions[axis_id].astype(F32)[:, None] * frequency[None, :]
        angle_list += [angles, angles]
        signs += [-1.0] * half_width + [1.0] * half_width
    angles = jnp.concatenate(angle_list, axis=1)
    return jnp.cos(angles), jnp.sin(angles) * jnp.array(signs, F32)[None, :]


def noise_level(step_value):
    level = 1.0 - step_value.astype(F32) / STEPS
    return 3.0 * level / (1.0 + 2.0 * level)


def per_device(
    text_tokens,
    image_tokens,
    extra_tokens,
    text_pos,
    image_pos,
    extra_pos,
    extra_counts,
    request_group,
    step_index,
    mod_table,
    final_table,
    qkv_weight,
    q_scale,
    k_scale,
    attn_out_weight,
    mlp_in_weight,
    mlp_out_weight,
    proj_weight,
    stencil,
    latent,
):
    group = lax.axis_index("wide")
    member = lax.axis_index("narrow")
    z, y = group // 4, group % 4
    chip, core = member // 2, member % 2
    step_here = step_index[request_group[group]]
    step_extra = step_index[step_index.shape[0] - 1]
    own_count = extra_counts[group * 8 + member]
    scalars = jnp.stack([step_here, step_extra, own_count]).astype(jnp.int32)
    text_own, image_own, extra_own = text_tokens[0], image_tokens[0], extra_tokens[0]

    out_weight = lax.all_gather(mlp_out_weight.T, "wide", axis=0, tiled=True)
    own = modulate(scalars, text_own, image_own, extra_own, mod_table)
    x = gather_rows(own)
    half = mlp_in_weight.shape[0] // 2
    pieces = collect(mlp_in_weight[:half], along_y, along_z) + collect(mlp_in_weight[half:], along_z, along_y)

    block_ids = jnp.arange(8, dtype=jnp.int32)
    sources = ((chip + block_ids % 4) % 4) * 2 + (core ^ (block_ids // 4))

    def by_block(array):
        chosen = (sources[:, None] == block_ids[None, :])[None, :, :, None]
        return jnp.sum(jnp.where(chosen, array[:, 0].reshape(3, 1, 8, -1), 0), axis=2)

    positions = jnp.concatenate([by_block(text_pos), by_block(image_pos), by_block(extra_pos)], axis=2)
    cosine, sine = rope_tables(positions.reshape(3, -1), 128)
    request_heads, extra_heads = project_heads(
        x, qkv_weight, jnp.stack([q_scale, k_scale]), cosine, sine, 8, extra_own.shape[0]
    )

    heads, slots = extra_heads.shape[1], extra_heads.shape[2]
    shared = extra_heads[1:].reshape(1, 2 * heads, slots, 128)
    before, after, far_first, far_last = ring(shared, along_y, lambda b: b[:, :heads], lambda b: b[:, heads:])
    far = jnp.concatenate([far_first, far_last], axis=1)
    quad = jnp.concatenate([shared, before, after, far], axis=0)
    key_pieces = (quad,) + ring(quad, along_z, lambda b: b[:2], lambda b: b[2:])
    attended = attend_request(request_heads)
    order = jnp.array(RING_ORDER, jnp.int32)
    groups = ((z + order) % 4)[:, None] * 4 + ((y + order) % 4)[None, :]
    owners = groups.reshape(16, 1) * 8 + sources[None, :]
    device_ids = jnp.arange(extra_counts.shape[0], dtype=jnp.int32)
    chosen = owners.reshape(-1)[:, None] == device_ids[None, :]
    counts = jnp.sum(jnp.where(chosen, extra_counts[None, :], 0), axis=1)
    slot_ids = jnp.arange(extra_own.shape[0], dtype=jnp.int32)
    live = (slot_ids[None, :] < counts[:, None]).astype(F32).reshape(1, -1)
    attended = attend_extra(extra_heads, live, attended, key_pieces, 8)

    act = hidden_units(jnp.stack([z, y]).astype(jnp.int32), x, pieces)
    chunks = 3
    columns = out_weight.shape[0] // chunks
    sums = []
    for chunk in range(chunks):
        part = output_part(act, out_weight, attended, attn_out_weight, chunk * columns, columns)
        sums.append(scatter_sum(part))
    text_out, image_out, extra_out, velocity = finish(
        scalars, text_own, image_own, extra_own, mod_table, final_table, proj_weight.T, sums
    )
    channels = proj_weight.shape[1]
    grid_width = latent.shape[2] // channels
    above = lax.ppermute(velocity[-grid_width:], "narrow", [(i, i + 1) for i in range(7)])
    below = lax.ppermute(velocity[:grid_width], "narrow", [(i + 1, i) for i in range(7)])
    delta = (noise_level(step_here + 1) - noise_level(step_here)).reshape(1)
    latent_next = smooth(
        delta, above, velocity, below, stencil, latent[0].reshape(-1, channels), grid_width
    )
    return (text_out[None], image_out[None], extra_out[None], latent_next.reshape(latent.shape))


def solution(mesh):
    return jax.shard_map(
        per_device,
        mesh=mesh,
        in_specs=(
            P("wide", "narrow", None),
            P("wide", "narrow", None),
            P("wide", "narrow", None),
            P(None, "wide", None),
            P(None, "wide", None),
            P(None, "wide", None),
            P(),
            P(),
            P(),
            P(),
            P(),
            P(None, None, "narrow"),
            P(),
            P(),
            P("narrow", None),
            P("wide", "narrow"),
            P("narrow", "wide"),
            P(),
            P(),
            P("wide", "narrow", None),
        ),
        out_specs=(
            P("wide", "narrow", None),
            P("wide", "narrow", None),
            P("wide", "narrow", None),
            P("wide", "narrow", None),
        ),
        check_vma=False,
    )
```

```python
import functools
import math

import jax
import jax.numpy as jnp
from jax import lax
from jax.experimental import pallas as pl
from jax.experimental.pallas import tpu as pltpu
from jax.sharding import PartitionSpec as P

STEPS = 4
EPSILON = 1e-06
ROPE_BASE = 10000.0
MIB = 1 << 20
F32 = jnp.float32
BF16 = jnp.bfloat16
NT = (((1,), (1,)), ((), ()))

VMEM = pl.BlockSpec(memory_space=pltpu.VMEM)
SMEM = pl.BlockSpec(memory_space=pltpu.SMEM)
ANY = pl.BlockSpec(memory_space=pl.ANY)


def section_widths(head_dim):
    return (head_dim // 8, 7 * head_dim // 16, 7 * head_dim // 16)


def layer_norm(values):
    centre = jnp.mean(values, axis=-1, keepdims=True)
    centred = values - centre
    spread = jnp.mean(centred * centred, axis=-1, keepdims=True)
    return centred * lax.rsqrt(spread + EPSILON)


def cost(flops, moved, exps=0):
    return pl.CostEstimate(flops=int(flops), bytes_accessed=int(moved), transcendentals=int(exps))


def wide_shift(dz, dy):
    return [(z * 4 + y, ((z + dz) % 4) * 4 + (y + dy) % 4) for z in range(4) for y in range(4)]


def chip_shift(step):
    return [(x * 2 + c, ((x + step) % 4) * 2 + c) for x in range(4) for c in range(2)]


CORE_SWAP = [(i, i ^ 1) for i in range(8)]
RING_ORDER = (0, -1, 1, 2)


def along_y(step):
    return wide_shift(0, step)


def along_z(step):
    return wide_shift(step, 0)


def wide(block, pairs):
    return lax.ppermute(block, "wide", pairs)


def output_layout():
    def places(part, *pairs):
        found = [(outer, inner) for outer, some in pairs for inner in some]
        return [(part, outer, inner) if part == 0 else (part, inner, outer) for outer, inner in found]

    low, high = RING_ORDER[:2], RING_ORDER[2:]
    first = [place for part in range(2) for place in places(part, (0, RING_ORDER))]
    first += [place for part in range(2) for place in places(part, (-1, low), (1, high))]
    return [first] + [places(part, (-1, high), (2, low), (1, low), (2, high)) for part in (1, 0)]


LAYOUT = output_layout()


def scatter_sum(partial):
    rows, columns = partial.shape[0] // 8, partial.shape[1]
    half = columns // 2
    other = lax.ppermute(partial[4 * rows :], "narrow", CORE_SWAP).astype(F32)
    pair = partial[: 4 * rows].astype(F32) + other
    far = pair[2 * rows : 3 * rows].astype(BF16)
    from_prv = lax.ppermute(far[:, :half], "narrow", chip_shift(1)).astype(F32)
    from_nxt = lax.ppermute(far[:, half:], "narrow", chip_shift(-1)).astype(F32)
    to_nxt = pair[rows : 2 * rows]
    to_prv = pair[3 * rows :]
    to_nxt = jnp.concatenate([to_nxt[:, :half] + from_prv, to_nxt[:, half:]], axis=1).astype(BF16)
    to_prv = jnp.concatenate([to_prv[:, :half], to_prv[:, half:] + from_nxt], axis=1).astype(BF16)
    one = lax.ppermute(to_nxt, "narrow", chip_shift(1))
    two = lax.ppermute(to_prv, "narrow", chip_shift(-1))
    return pair[:rows], one, two


def steps_of(ids, request_group, step_index):
    return step_index[request_group[ids[0]]], step_index[step_index.shape[0] - 1]


def modulate_kernel(ids, request_group, step_index, text, image, extra, mod_table, out):
    here, there = steps_of(ids, request_group, step_index)
    shift, scale = mod_table[here, 0:1, :], mod_table[here, 1:2, :]
    row = 0
    for ref in (text, image):
        rows = ref.shape[0]
        out[row : row + rows, :] = (layer_norm(ref[...].astype(F32)) * (1.0 + scale) + shift).astype(BF16)
        row += rows
    shift, scale = mod_table[there, 0:1, :], mod_table[there, 1:2, :]
    rows = extra.shape[0]
    out[row : row + rows, :] = (layer_norm(extra[...].astype(F32)) * (1.0 + scale) + shift).astype(BF16)


def modulate(scalars, text, image, extra, mod_table):
    rows = text.shape[0] + image.shape[0] + extra.shape[0]
    return pl.pallas_call(
        modulate_kernel,
        out_shape=jax.ShapeDtypeStruct((rows, text.shape[1]), BF16),
        in_specs=[SMEM] * 3 + [VMEM] * 4,
        out_specs=VMEM,
        compiler_params=pltpu.CompilerParams(vmem_limit_bytes=8 * MIB),
        cost_estimate=cost(1e6, 2 * MIB),
    )(*scalars, text, image, extra, mod_table)


def partner_of(values):
    lane = lax.broadcasted_iota(jnp.int32, values.shape, 1)
    width = values.shape[1]
    result = None
    offset = 0
    rolled = {}
    for section in section_widths(width):
        half = section // 2
        for amount, start in ((width - half, offset), (half, offset + half)):
            if amount not in rolled:
                rolled[amount] = pltpu.roll(values, amount, 1)
            result = rolled[amount] if result is None else jnp.where(lane >= start, rolled[amount], result)
        offset += section
    return result


def heads_kernel(blocks, own, x, weight, gains, cosine, sine, request, extra):
    which = pl.program_id(0)
    total = x.shape[0]
    rows = total // blocks
    taken = rows - own
    step = 4 * rows
    heads = weight.shape[2] // 128

    def tile(index, carry):
        start = pl.multiple_of(index * step, 32)
        acc = jnp.dot(x[pl.ds(start, step), :], weight[0], preferred_element_type=F32)

        def put(head, values):
            for part in range(4):
                first = part * rows
                block = 4 * index + part
                request[0, head, pl.ds(pl.multiple_of(block * taken, 32), taken), :] = values[first : first + taken]
                extra[0, head, pl.ds(pl.multiple_of(block * own, 16), own), :] = values[first + taken : first + rows]

        @pl.when(which < 2)
        def _():
            gain = gains[pl.ds(which, 1), :]
            cos = cosine[pl.ds(start, step), :]
            sin = sine[pl.ds(start, step), :]
            for head in range(heads):
                part = acc[:, head * 128 : (head + 1) * 128]
                square = jnp.mean(part * part, axis=1, keepdims=True)
                part = part * lax.rsqrt(square + EPSILON) * gain
                put(head, (part * cos + partner_of(part) * sin).astype(BF16))

        @pl.when(which == 2)
        def _():
            for head in range(heads):
                put(head, acc[:, head * 128 : (head + 1) * 128].astype(BF16))

        return carry

    lax.fori_loop(0, total // step, tile, 0)


def project_heads(x, weight, gains, cosine, sine, blocks, own):
    total, width = x.shape
    heads = weight.shape[2] // 128
    extra = blocks * own
    request = total - extra
    return pl.pallas_call(
        functools.partial(heads_kernel, blocks, own),
        grid=(3,),
        out_shape=(
            jax.ShapeDtypeStruct((3, heads, request, 128), BF16),
            jax.ShapeDtypeStruct((3, heads, extra, 128), BF16),
        ),
        in_specs=[
            VMEM,
            pl.BlockSpec((1, width, weight.shape[2]), lambda i: (i, 0, 0)),
            VMEM,
            VMEM,
            VMEM,
        ],
        out_specs=(
            pl.BlockSpec((1, heads, request, 128), lambda i: (i, 0, 0, 0)),
            pl.BlockSpec((1, heads, extra, 128), lambda i: (i, 0, 0, 0)),
        ),
        compiler_params=pltpu.CompilerParams(vmem_limit_bytes=32 * MIB),
        cost_estimate=cost(6 * total * width * weight.shape[2], 16 * MIB),
    )(x, weight, gains, cosine, sine)


def weigh(query, keys, values, live):
    scores = lax.dot_general(query, keys, NT, preferred_element_type=F32)
    weights = jnp.exp(scores * (1.0 / math.sqrt(query.shape[1])))
    if live is not None:
        weights = jnp.where(live, weights, 0.0)
    running = jnp.sum(weights, axis=1, keepdims=True)
    total = jnp.dot(weights.astype(BF16), values, preferred_element_type=F32)
    return (total / running).astype(BF16)


def request_kernel(query, keys, values, out):
    step = 256
    for start in range(0, query.shape[2], step):
        out[start : start + step, :] = weigh(query[0, 0, start : start + step, :], keys[0, 0], values[0, 0], None)


def attend_request(heads):
    count, rows = heads.shape[1], heads.shape[2]

    def block(which):
        return pl.BlockSpec((1, 1, rows, 128), lambda h: (which, h, 0, 0))

    return pl.pallas_call(
        request_kernel,
        grid=(count,),
        out_shape=jax.ShapeDtypeStruct((rows, count * 128), BF16),
        in_specs=[block(0), block(1), block(2)],
        out_specs=pl.BlockSpec((rows, 128), lambda h: (0, h)),
        compiler_params=pltpu.CompilerParams(vmem_limit_bytes=16 * MIB),
        cost_estimate=cost(4 * count * rows * rows * 128, 5 * MIB, count * rows * rows),
    )(heads, heads, heads)


def extra_kernel(blocks, query, live, done, *refs):
    keys, values, out = refs[:5], refs[5:10], refs[10]
    every_key = jnp.concatenate([ref[i, 0] for ref in keys for i in range(ref.shape[0])], axis=0)
    every_value = jnp.concatenate([ref[i, 0] for ref in values for i in range(ref.shape[0])], axis=0)
    attended = weigh(query[0, 0], every_key, every_value, live[...] > 0)
    taken, own = done.shape[0] // blocks, attended.shape[0] // blocks
    rows = taken + own
    for block in range(blocks):
        out[block * rows : block * rows + taken, :] = done[block * taken : (block + 1) * taken, :]
        out[block * rows + taken : (block + 1) * rows, :] = attended[block * own : (block + 1) * own, :]


def attend_extra(heads, live, done, pieces, blocks):
    count, rows = heads.shape[1], heads.shape[2]

    def pair(first):
        return [
            pl.BlockSpec((piece.shape[0], 1, rows, 128), lambda h: (0, first + h, 0, 0)) for piece in pieces
        ]

    total = done.shape[0] + rows
    return pl.pallas_call(
        functools.partial(extra_kernel, blocks),
        grid=(count,),
        out_shape=jax.ShapeDtypeStruct((total, count * 128), BF16),
        in_specs=[
            pl.BlockSpec((1, 1, rows, 128), lambda h: (0, h, 0, 0)),
            pl.BlockSpec(live.shape, lambda h: (0, 0)),
            pl.BlockSpec((done.shape[0], 128), lambda h: (0, h)),
        ]
        + pair(0)
        + pair(count),
        out_specs=pl.BlockSpec((total, 128), lambda h: (0, h)),
        compiler_params=pltpu.CompilerParams(vmem_limit_bytes=16 * MIB),
        cost_estimate=cost(4 * count * rows * live.shape[1] * 128, 5 * MIB, count * rows * live.shape[1]),
    )(heads, live, done, *pieces, *pieces)


def gelu(values):
    inner = math.sqrt(2.0 / math.pi) * (values + 0.044715 * (values * values * values))
    return values * (0.5 * (1.0 + jnp.tanh(inner)))


def hidden_kernel(x, weight, out):
    out[...] = gelu(jnp.dot(x[...], weight[...], preferred_element_type=F32)).astype(BF16)


def hidden_units(x, weight, step=256):
    rows, width = x.shape
    units = weight.shape[1]
    return pl.pallas_call(
        hidden_kernel,
        grid=(units // step,),
        out_shape=jax.ShapeDtypeStruct((rows, units), BF16),
        in_specs=[pl.BlockSpec((rows, width), lambda i: (0, 0)), pl.BlockSpec((width, step), lambda i: (0, i))],
        out_specs=pl.BlockSpec((rows, step), lambda i: (0, i)),
        compiler_params=pltpu.CompilerParams(vmem_limit_bytes=40 * MIB),
        cost_estimate=cost(2 * rows * width * units, 18 * MIB, rows * units),
    )(x, weight)


def output_kernel(chunk, ids, act, attended, attn_weight, *refs):
    pieces, out, weight, attn_part = refs[:-3], refs[-3], refs[-2], refs[-1]
    z, y = ids[0] // 4, ids[0] % 4
    row = 0
    for piece in pieces:
        rows = piece.shape[0]
        weight[row : row + rows, :] = piece[...]
        row += rows
    half = row // len(LAYOUT[chunk])
    for index, (part, dz, dy) in enumerate(LAYOUT[chunk]):
        group = lax.rem(z + (dz + 4), 4) * 4 + lax.rem(y + (dy + 4), 4)
        start = pl.multiple_of(group * (2 * half) + part * half, 32)
        attn_part[index * half : (index + 1) * half, :] = attn_weight[pl.ds(start, half), :]
    step = 256

    def tile(index, carry):
        columns = pl.ds(pl.multiple_of(index * step, step), step)
        acc = lax.dot_general(act[...], weight[columns, :], NT, preferred_element_type=F32)
        acc = acc + lax.dot_general(attended[...], attn_part[columns, :], NT, preferred_element_type=F32)
        out[:, columns] = acc.astype(BF16)
        return carry

    lax.fori_loop(0, row // step, tile, 0)


def output_part(chunk, ids, act, attended, attn_weight, pieces):
    rows, units = act.shape
    columns = sum(piece.shape[0] for piece in pieces)
    return pl.pallas_call(
        functools.partial(output_kernel, chunk),
        out_shape=jax.ShapeDtypeStruct((rows, columns), BF16),
        in_specs=[SMEM] + [VMEM] * (3 + len(pieces)),
        out_specs=VMEM,
        scratch_shapes=[pltpu.VMEM((columns, units), BF16), pltpu.VMEM((columns, attended.shape[1]), BF16)],
        compiler_params=pltpu.CompilerParams(vmem_limit_bytes=24 * MIB),
        cost_estimate=cost(2 * rows * columns * (units + attended.shape[1]), 8 * MIB),
    )(ids, act, attended, attn_weight, *pieces)


def split_three(first, second, third):
    lane = lax.broadcasted_iota(jnp.int32, first.shape, 1)
    return (
        first,
        jnp.where(lane < 32, pltpu.roll(first, 32, 1), pltpu.roll(second, 32, 1)),
        jnp.where(lane < 64, pltpu.roll(second, 64, 1), pltpu.roll(third, 64, 1)),
        pltpu.roll(third, 96, 1),
    )


def join_four(one, two, three, four):
    lane = lax.broadcasted_iota(jnp.int32, one.shape, 1)
    two, three, four = pltpu.roll(two, 96, 1), pltpu.roll(three, 64, 1), pltpu.roll(four, 32, 1)
    return jnp.concatenate(
        [jnp.where(lane < 96, one, two), jnp.where(lane < 64, two, three), jnp.where(lane < 32, three, four)], axis=1
    )


def finish_kernel(
    chunks, ids, request_group, step_index, counts, slot_of, text, image, extra, mod_table, final_table, proj, *refs
):
    sums, (text_out, image_out, extra_out, velocity, hidden, parts) = refs[: 3 * chunks], refs[3 * chunks :]
    here, there = steps_of(ids, request_group, step_index)
    count = counts[ids[0] * 8 + ids[1]]
    z, y = ids[0] // 4, ids[0] % 4
    rows_text, rows_image = text.shape[0], image.shape[0]
    filled = 0
    for chunk in range(chunks):
        own, one, two = sums[3 * chunk : 3 * chunk + 3]
        total = own[...] + one[...].astype(F32) + two[...].astype(F32)
        for half in range(total.shape[1] // 384):
            tiles = [total[:, (3 * half + i) * 128 : (3 * half + i + 1) * 128] for i in range(3)]
            for index, part in enumerate(split_three(*tiles)):
                parts[filled + 4 * half + index] = part
        filled += 4 * (total.shape[1] // 384)
    width = 384
    for pair in range(8):
        found = []
        for group in (2 * pair, 2 * pair + 1):
            dz = lax.rem(group // 4 - z + 4, 4)
            dy = lax.rem(group % 4 - y + 4, 4)
            found += [parts[slot_of[part * 16 + dz * 4 + dy]] for part in range(2)]
        total = join_four(*found)
        columns = slice(pair * width, (pair + 1) * width)
        gate = mod_table[here, 2:3, columns]
        text_out[:, columns] = (text[:, columns].astype(F32) + gate * total[:rows_text]).astype(BF16)
        states = image[:, columns].astype(F32) + gate * total[rows_text : rows_text + rows_image]
        hidden[:, columns] = states
        image_out[:, columns] = states.astype(BF16)
        gate = mod_table[there, 2:3, columns]
        slots = extra[:, columns].astype(F32) + gate * total[rows_text + rows_image :]
        live = lax.broadcasted_iota(jnp.int32, slots.shape, 0) < count
        extra_out[:, columns] = jnp.where(live, slots, 0.0).astype(BF16)
    shift, scale = final_table[here, 0:1, :], final_table[here, 1:2, :]
    normed = (layer_norm(hidden[...]) * (1.0 + scale) + shift).astype(BF16)
    velocity[...] = lax.dot_general(normed, proj[...], NT, preferred_element_type=F32)


def finish(scalars, text, image, extra, mod_table, final_table, proj, sums):
    width = text.shape[1]
    flat = [part for chunk in sums for part in chunk]
    slot_of = [0] * 32
    for index, (part, dz, dy) in enumerate(place for chunk in LAYOUT for place in chunk):
        slot_of[part * 16 + (dz % 4) * 4 + dy % 4] = index
    rows = flat[0].shape[0]
    return pl.pallas_call(
        functools.partial(finish_kernel, len(sums)),
        out_shape=(
            jax.ShapeDtypeStruct(text.shape, BF16),
            jax.ShapeDtypeStruct(image.shape, BF16),
            jax.ShapeDtypeStruct(extra.shape, BF16),
            jax.ShapeDtypeStruct((image.shape[0], proj.shape[0]), F32),
        ),
        in_specs=[SMEM] * 5 + [VMEM] * (6 + len(flat)),
        out_specs=(VMEM,) * 4,
        scratch_shapes=[pltpu.VMEM((image.shape[0], width), F32), pltpu.VMEM((32, rows, 128), F32)],
        compiler_params=pltpu.CompilerParams(vmem_limit_bytes=20 * MIB),
        cost_estimate=cost(1e7, 5 * MIB),
    )(*scalars, jnp.array(slot_of, jnp.int32), text, image, extra, mod_table, final_table, proj, *flat)


def smooth_kernel(columns, delta, above, middle, below, stencil, latent, out):
    rows = middle.shape[0]
    cells = jnp.concatenate([above[...], middle[...], below[...]], axis=0)
    column = lax.rem(lax.broadcasted_iota(jnp.int32, middle.shape, 0), columns)
    total = jnp.zeros(middle.shape, F32)
    for row_tap in range(3):
        band = cells[row_tap * columns : row_tap * columns + rows]
        for col_tap in range(3):
            moved = band if col_tap == 1 else pltpu.roll(band, (1 - col_tap) % rows, 0)
            place = column + (col_tap - 1)
            moved = jnp.where((place >= 0) & (place < columns), moved, 0.0)
            tap = 3 * row_tap + col_tap
            total = total + stencil[tap : tap + 1, :] * moved
    out[...] = latent[...] + delta[0] * total


def smooth(delta, above, middle, below, stencil, latent, columns):
    return pl.pallas_call(
        functools.partial(smooth_kernel, columns),
        out_shape=jax.ShapeDtypeStruct(middle.shape, F32),
        in_specs=[SMEM] + [VMEM] * 5,
        out_specs=VMEM,
        cost_estimate=cost(1e5, 1e5),
    )(delta, above, middle, below, stencil, latent)


def rope_tables(positions, head_dim):
    angle_list, signs = [], []
    for axis_id, section in enumerate(section_widths(head_dim)):
        half_width = section // 2
        exponent = -2.0 * jnp.arange(half_width, dtype=F32) / section
        frequency = jnp.power(F32(ROPE_BASE), exponent)
        angles = positions[axis_id].astype(F32)[:, None] * frequency[None, :]
        angle_list += [angles, angles]
        signs += [-1.0] * half_width + [1.0] * half_width
    angles = jnp.concatenate(angle_list, axis=1)
    return jnp.cos(angles), jnp.sin(angles) * jnp.array(signs, F32)[None, :]


def noise_level(step_value):
    level = 1.0 - step_value.astype(F32) / STEPS
    return 3.0 * level / (1.0 + 2.0 * level)


def per_device(
    text_tokens,
    image_tokens,
    extra_tokens,
    text_pos,
    image_pos,
    extra_pos,
    extra_counts,
    request_group,
    step_index,
    mod_table,
    final_table,
    qkv_weight,
    q_scale,
    k_scale,
    attn_out_weight,
    mlp_in_weight,
    mlp_out_weight,
    proj_weight,
    stencil,
    latent,
):
    group = lax.axis_index("wide")
    member = lax.axis_index("narrow")
    z, y = group // 4, group % 4
    chip, core = member // 2, member % 2
    ids = jnp.stack([group, member]).astype(jnp.int32)
    scalars = (ids, request_group, step_index)
    text_own, image_own, extra_own = text_tokens[0], image_tokens[0], extra_tokens[0]

    hidden_weight = lax.all_gather(mlp_in_weight, "wide", axis=0, tiled=True)
    own = modulate(scalars, text_own, image_own, extra_own, mod_table)

    together = lax.optimization_barrier
    out_weight = mlp_out_weight.T
    size = out_weight.shape[0] // 2
    routes = ((along_y, along_z), (along_z, along_y))
    mine = [out_weight[:size], out_weight[size:]]
    near = [wide(mine[i], routes[i][0](step)) for i in range(2) for step in (1, -1)]
    *near, own = together((*near, own))

    def swap(block):
        return lax.ppermute(block, "narrow", CORE_SWAP)

    nxt = lax.ppermute(own, "narrow", chip_shift(-1))
    prv = lax.ppermute(own, "narrow", chip_shift(1))
    own_swapped = swap(own)
    far = [wide(near[2 * i], routes[i][0](1)) for i in range(2)]
    *far, nxt, prv, own_swapped = together((*far, nxt, prv, own_swapped))

    cut = own.shape[0] // 2
    far_a = lax.ppermute(nxt[:cut], "narrow", chip_shift(-1))
    far_b = lax.ppermute(prv[cut:], "narrow", chip_shift(1))
    near_swapped = swap(jnp.concatenate([nxt, prv], axis=0))
    low = [jnp.concatenate([mine[i], near[2 * i]], axis=0) for i in range(2)]
    high = [jnp.concatenate([near[2 * i + 1], far[i]], axis=0) for i in range(2)]
    early = [wide(low[0], routes[0][1](1)), wide(high[0], routes[0][1](-1))]
    far_a, far_b, near_swapped, low[1], high[1] = together((far_a, far_b, near_swapped, low[1], high[1]))
    across = jnp.concatenate([far_a, far_b], axis=0)
    early += [wide(low[1], routes[1][1](1)), wide(high[1], routes[1][1](-1))]
    rows = own.shape[0]
    x = jnp.concatenate(
        [own, nxt, across, prv, own_swapped, near_swapped[:rows], swap(across), near_swapped[rows:]], axis=0
    )

    block_ids = jnp.arange(8, dtype=jnp.int32)
    sources = ((chip + block_ids % 4) % 4) * 2 + (core ^ (block_ids // 4))

    def by_block(array):
        chosen = (sources[:, None] == block_ids[None, :])[None, :, :, None]
        return jnp.sum(jnp.where(chosen, array[:, 0].reshape(3, 1, 8, -1), 0), axis=2)

    positions = jnp.concatenate([by_block(text_pos), by_block(image_pos), by_block(extra_pos)], axis=2)
    cosine, sine = rope_tables(positions.reshape(3, -1), 128)
    request_heads, extra_heads = project_heads(
        x, qkv_weight, jnp.stack([q_scale, k_scale]), cosine, sine, 8, extra_own.shape[0]
    )

    heads, slots = extra_heads.shape[1], extra_heads.shape[2]
    extra_heads, *early = together((extra_heads, *early))
    shared = extra_heads[1:].reshape(1, 2 * heads, slots, 128)
    before, after = wide(shared, along_y(1)), wide(shared, along_y(-1))

    def rest(i):
        ahead = jnp.concatenate([high[i], early[2 * i]], axis=0)
        back = jnp.concatenate([low[i], early[2 * i + 1]], axis=0)
        return ahead, back

    ahead, back = rest(1)
    before, after, ahead, back = together((before, after, ahead, back))
    first, second = wide(before[:, :heads], along_y(1)), wide(after[:, heads:], along_y(-1))
    late = [[wide(ahead, routes[1][1](1)), wide(back, routes[1][1](-1))]]
    attended = attend_request(request_heads)
    key_quad = jnp.concatenate([shared, before, after, jnp.concatenate([first, second], axis=1)], axis=0)
    above, below = wide(key_quad, along_z(1)), wide(key_quad, along_z(-1))
    ahead, back = rest(0)
    above, below, ahead, back, x, attended = together((above, below, ahead, back, x, attended))
    first, second = wide(above[:2], along_z(1)), wide(below[2:], along_z(-1))
    late.append([wide(ahead, routes[0][1](1)), wide(back, routes[0][1](-1))])
    act = hidden_units(x, hidden_weight)
    act, first, second = together((act, first, second))
    key_pieces = (key_quad, above, below, first, second)
    order = jnp.array(RING_ORDER, jnp.int32)
    groups = ((z + order) % 4)[:, None] * 4 + ((y + order) % 4)[None, :]
    owners = groups.reshape(16, 1) * 8 + sources[None, :]
    device_ids = jnp.arange(extra_counts.shape[0], dtype=jnp.int32)
    chosen = owners.reshape(-1)[:, None] == device_ids[None, :]
    counts = jnp.sum(jnp.where(chosen, extra_counts[None, :], 0), axis=1)
    slot_ids = jnp.arange(extra_own.shape[0], dtype=jnp.int32)
    live = (slot_ids[None, :] < counts[:, None]).astype(F32).reshape(1, -1)
    attended = attend_extra(extra_heads, live, attended, key_pieces, 8)

    attn_weight = attn_out_weight.T
    chunks = [low[:1] + high[:1] + low[1:] + high[1:] + early] + late
    sums = [scatter_sum(output_part(i, ids, act, attended, attn_weight, pieces)) for i, pieces in enumerate(chunks)]
    text_out, image_out, extra_out, velocity = finish(
        (*scalars, extra_counts), text_own, image_own, extra_own, mod_table, final_table, proj_weight.T, sums
    )
    channels = proj_weight.shape[1]
    grid_width = latent.shape[2] // channels
    above = lax.ppermute(velocity[-grid_width:], "narrow", [(i, i + 1) for i in range(7)])
    below = lax.ppermute(velocity[:grid_width], "narrow", [(i + 1, i) for i in range(7)])
    step_here = step_index[request_group[group]]
    delta = (noise_level(step_here + 1) - noise_level(step_here)).reshape(1)
    latent_next = smooth(
        delta, above, velocity, below, stencil, latent[0].reshape(-1, channels), grid_width
    )
    return (text_out[None], image_out[None], extra_out[None], latent_next.reshape(latent.shape))


def solution(mesh):
    return jax.shard_map(
        per_device,
        mesh=mesh,
        in_specs=(
            P("wide", "narrow", None),
            P("wide", "narrow", None),
            P("wide", "narrow", None),
            P(None, "wide", None),
            P(None, "wide", None),
            P(None, "wide", None),
            P(),
            P(),
            P(),
            P(),
            P(),
            P(None, None, "narrow"),
            P(),
            P(),
            P("narrow", None),
            P("wide", "narrow"),
            P("narrow", "wide"),
            P(),
            P(),
            P("wide", "narrow", None),
        ),
        out_specs=(
            P("wide", "narrow", None),
            P("wide", "narrow", None),
            P("wide", "narrow", None),
            P("wide", "narrow", None),
        ),
        check_vma=False,
    )
```

```python
import functools
import math

import jax
import jax.numpy as jnp
from jax import lax
from jax.experimental import pallas as pl
from jax.experimental.pallas import tpu as pltpu
from jax.sharding import PartitionSpec as P

STEPS = 4
EPSILON = 1e-06
ROPE_BASE = 10000.0
MIB = 1 << 20
F32 = jnp.float32
BF16 = jnp.bfloat16
NT = (((1,), (1,)), ((), ()))

VMEM = pl.BlockSpec(memory_space=pltpu.VMEM)
SMEM = pl.BlockSpec(memory_space=pltpu.SMEM)
ANY = pl.BlockSpec(memory_space=pl.ANY)


def section_widths(head_dim):
    return (head_dim // 8, 7 * head_dim // 16, 7 * head_dim // 16)


def layer_norm(values):
    centre = jnp.mean(values, axis=-1, keepdims=True)
    centred = values - centre
    spread = jnp.mean(centred * centred, axis=-1, keepdims=True)
    return centred * lax.rsqrt(spread + EPSILON)


def cost(flops, moved, exps=0):
    return pl.CostEstimate(flops=int(flops), bytes_accessed=int(moved), transcendentals=int(exps))


def wide_shift(dz, dy):
    return [(z * 4 + y, ((z + dz) % 4) * 4 + (y + dy) % 4) for z in range(4) for y in range(4)]


def chip_shift(step):
    return [(x * 2 + c, ((x + step) % 4) * 2 + c) for x in range(4) for c in range(2)]


CORE_SWAP = [(i, i ^ 1) for i in range(8)]
RING_ORDER = (0, -1, 1, 2)


def along_y(step):
    return wide_shift(0, step)


def along_z(step):
    return wide_shift(step, 0)


def wide(block, pairs):
    return lax.ppermute(block, "wide", pairs)


def output_layout():
    def places(part, *pairs):
        found = [(outer, inner) for outer, some in pairs for inner in some]
        return [(part, outer, inner) if part == 0 else (part, inner, outer) for outer, inner in found]

    low, high = RING_ORDER[:2], RING_ORDER[2:]
    first = [place for part in range(2) for place in places(part, (0, RING_ORDER))]
    first += [place for part in range(2) for place in places(part, (-1, low), (1, high))]
    return [first] + [places(part, (-1, high), (2, low), (1, low), (2, high)) for part in (1, 0)]


LAYOUT = output_layout()


def to_core(partial):
    return lax.ppermute(partial[partial.shape[0] // 2 :], "narrow", CORE_SWAP)


def to_far(partial, other):
    rows, half = partial.shape[0] // 8, partial.shape[1] // 2
    pair = partial[: 4 * rows].astype(F32) + other.astype(F32)
    far = pair[2 * rows : 3 * rows].astype(BF16)
    from_prv = lax.ppermute(far[:, :half], "narrow", chip_shift(1))
    from_nxt = lax.ppermute(far[:, half:], "narrow", chip_shift(-1))
    return pair, from_prv, from_nxt


def to_near(pair, from_prv, from_nxt):
    rows, half = pair.shape[0] // 4, pair.shape[1] // 2
    to_nxt, to_prv = pair[rows : 2 * rows], pair[3 * rows :]
    to_nxt = jnp.concatenate([to_nxt[:, :half] + from_prv.astype(F32), to_nxt[:, half:]], axis=1).astype(BF16)
    to_prv = jnp.concatenate([to_prv[:, :half], to_prv[:, half:] + from_nxt.astype(F32)], axis=1).astype(BF16)
    one = lax.ppermute(to_nxt, "narrow", chip_shift(1))
    two = lax.ppermute(to_prv, "narrow", chip_shift(-1))
    return pair[:rows], one, two


def steps_of(ids, request_group, step_index):
    return step_index[request_group[ids[0]]], step_index[step_index.shape[0] - 1]


def modulate_kernel(ids, request_group, step_index, text, image, extra, mod_table, out):
    here, there = steps_of(ids, request_group, step_index)
    shift, scale = mod_table[here, 0:1, :], mod_table[here, 1:2, :]
    row = 0
    for ref in (text, image):
        rows = ref.shape[0]
        out[row : row + rows, :] = (layer_norm(ref[...].astype(F32)) * (1.0 + scale) + shift).astype(BF16)
        row += rows
    shift, scale = mod_table[there, 0:1, :], mod_table[there, 1:2, :]
    rows = extra.shape[0]
    out[row : row + rows, :] = (layer_norm(extra[...].astype(F32)) * (1.0 + scale) + shift).astype(BF16)


def modulate(scalars, text, image, extra, mod_table):
    rows = text.shape[0] + image.shape[0] + extra.shape[0]
    return pl.pallas_call(
        modulate_kernel,
        out_shape=jax.ShapeDtypeStruct((rows, text.shape[1]), BF16),
        in_specs=[SMEM] * 3 + [VMEM] * 4,
        out_specs=VMEM,
        compiler_params=pltpu.CompilerParams(vmem_limit_bytes=8 * MIB),
        cost_estimate=cost(1e6, 2 * MIB),
    )(*scalars, text, image, extra, mod_table)


def partner_of(values):
    lane = lax.broadcasted_iota(jnp.int32, values.shape, 1)
    width = values.shape[1]
    result = None
    offset = 0
    rolled = {}
    for section in section_widths(width):
        half = section // 2
        for amount, start in ((width - half, offset), (half, offset + half)):
            if amount not in rolled:
                rolled[amount] = pltpu.roll(values, amount, 1)
            result = rolled[amount] if result is None else jnp.where(lane >= start, rolled[amount], result)
        offset += section
    return result


def heads_kernel(blocks, own, x, weight, gains, cosine, sine, request, extra):
    which = pl.program_id(0)
    total = x.shape[0]
    rows = total // blocks
    taken = rows - own
    step = 4 * rows
    heads = weight.shape[2] // 128

    plain = which == 2
    gain = gains[pl.ds(jnp.minimum(which, 1), 1), :]
    for start in range(0, total, step):
        acc = jnp.dot(x[start : start + step, :], weight[0], preferred_element_type=F32)
        cos = cosine[start : start + step, :]
        sin = sine[start : start + step, :]
        for head in range(heads):
            part = acc[:, head * 128 : (head + 1) * 128]
            square = jnp.mean(part * part, axis=1, keepdims=True)
            normed = part * lax.rsqrt(square + EPSILON) * gain
            values = jnp.where(plain, part, normed * cos + partner_of(normed) * sin).astype(BF16)
            for index in range(step // rows):
                first, block = index * rows, start // rows + index
                request[0, head, block * taken : (block + 1) * taken, :] = values[first : first + taken]
                extra[0, head, block * own : (block + 1) * own, :] = values[first + taken : first + rows]


def project_heads(x, weight, gains, cosine, sine, blocks, own):
    total, width = x.shape
    heads = weight.shape[2] // 128
    extra = blocks * own
    request = total - extra
    return pl.pallas_call(
        functools.partial(heads_kernel, blocks, own),
        grid=(3,),
        out_shape=(
            jax.ShapeDtypeStruct((3, heads, request, 128), BF16),
            jax.ShapeDtypeStruct((3, heads, extra, 128), BF16),
        ),
        in_specs=[
            VMEM,
            pl.BlockSpec((1, width, weight.shape[2]), lambda i: (i, 0, 0)),
            VMEM,
            VMEM,
            VMEM,
        ],
        out_specs=(
            pl.BlockSpec((1, heads, request, 128), lambda i: (i, 0, 0, 0)),
            pl.BlockSpec((1, heads, extra, 128), lambda i: (i, 0, 0, 0)),
        ),
        compiler_params=pltpu.CompilerParams(vmem_limit_bytes=32 * MIB),
        cost_estimate=cost(6 * total * width * weight.shape[2], 16 * MIB),
    )(x, weight, gains, cosine, sine)


def weigh(query, keys, values, live):
    scores = lax.dot_general(query, keys, NT, preferred_element_type=F32)
    weights = jnp.exp(scores * (1.0 / math.sqrt(query.shape[1])))
    if live is not None:
        weights = jnp.where(live, weights, 0.0)
    running = jnp.sum(weights, axis=1, keepdims=True)
    total = jnp.dot(weights.astype(BF16), values, preferred_element_type=F32)
    return (total / running).astype(BF16)


def request_kernel(query, keys, values, out):
    step = 256
    for start in range(0, query.shape[2], step):
        out[start : start + step, :] = weigh(query[0, 0, start : start + step, :], keys[0, 0], values[0, 0], None)


def attend_request(heads):
    count, rows = heads.shape[1], heads.shape[2]

    def block(which):
        return pl.BlockSpec((1, 1, rows, 128), lambda h: (which, h, 0, 0))

    return pl.pallas_call(
        request_kernel,
        grid=(count,),
        out_shape=jax.ShapeDtypeStruct((rows, count * 128), BF16),
        in_specs=[block(0), block(1), block(2)],
        out_specs=pl.BlockSpec((rows, 128), lambda h: (0, h)),
        compiler_params=pltpu.CompilerParams(vmem_limit_bytes=16 * MIB),
        cost_estimate=cost(4 * count * rows * rows * 128, 5 * MIB, count * rows * rows),
    )(heads, heads, heads)


def extra_kernel(blocks, query, live, done, *refs):
    keys, values, out = refs[:5], refs[5:10], refs[10]
    every_key = jnp.concatenate([ref[i, 0] for ref in keys for i in range(ref.shape[0])], axis=0)
    every_value = jnp.concatenate([ref[i, 0] for ref in values for i in range(ref.shape[0])], axis=0)
    attended = weigh(query[0, 0], every_key, every_value, live[...] > 0)
    taken, own = done.shape[0] // blocks, attended.shape[0] // blocks
    rows = taken + own
    for block in range(blocks):
        out[block * rows : block * rows + taken, :] = done[block * taken : (block + 1) * taken, :]
        out[block * rows + taken : (block + 1) * rows, :] = attended[block * own : (block + 1) * own, :]


def attend_extra(heads, live, done, pieces, blocks):
    count, rows = heads.shape[1], heads.shape[2]

    def pair(first):
        return [
            pl.BlockSpec((piece.shape[0], 1, rows, 128), lambda h: (0, first + h, 0, 0)) for piece in pieces
        ]

    total = done.shape[0] + rows
    return pl.pallas_call(
        functools.partial(extra_kernel, blocks),
        grid=(count,),
        out_shape=jax.ShapeDtypeStruct((total, count * 128), BF16),
        in_specs=[
            pl.BlockSpec((1, 1, rows, 128), lambda h: (0, h, 0, 0)),
            pl.BlockSpec(live.shape, lambda h: (0, 0)),
            pl.BlockSpec((done.shape[0], 128), lambda h: (0, h)),
        ]
        + pair(0)
        + pair(count),
        out_specs=pl.BlockSpec((total, 128), lambda h: (0, h)),
        compiler_params=pltpu.CompilerParams(vmem_limit_bytes=16 * MIB),
        cost_estimate=cost(4 * count * rows * live.shape[1] * 128, 5 * MIB, count * rows * live.shape[1]),
    )(heads, live, done, *pieces, *pieces)


def gelu(values):
    root = math.sqrt(2.0 / math.pi)
    half = 0.5 * values
    return half + half * jnp.tanh(values * (root + (root * 0.044715) * (values * values)))


def hidden_kernel(x, weight, out):
    rows = x.shape[0] // 2
    for start in (0, rows):
        acc = jnp.dot(x[start : start + rows, :], weight[...], preferred_element_type=F32)
        out[start : start + rows, :] = gelu(acc).astype(BF16)


def hidden_units(x, weight, step=256):
    rows, width = x.shape
    units = weight.shape[1]
    return pl.pallas_call(
        hidden_kernel,
        grid=(units // step,),
        out_shape=jax.ShapeDtypeStruct((rows, units), BF16),
        in_specs=[pl.BlockSpec((rows, width), lambda i: (0, 0)), pl.BlockSpec((width, step), lambda i: (0, i))],
        out_specs=pl.BlockSpec((rows, step), lambda i: (0, i)),
        compiler_params=pltpu.CompilerParams(vmem_limit_bytes=40 * MIB),
        cost_estimate=cost(2 * rows * width * units, 18 * MIB, rows * units),
    )(x, weight)


def output_kernel(chunk, ids, act, attended, attn_weight, *refs):
    pieces, out, weight, attn_part = refs[:-3], refs[-3], refs[-2], refs[-1]
    z, y = ids[0] // 4, ids[0] % 4
    row = 0
    for piece in pieces:
        rows = piece.shape[0]
        weight[row : row + rows, :] = piece[...]
        row += rows
    half = row // len(LAYOUT[chunk])
    for index, (part, dz, dy) in enumerate(LAYOUT[chunk]):
        group = lax.rem(z + (dz + 4), 4) * 4 + lax.rem(y + (dy + 4), 4)
        start = pl.multiple_of(group * (2 * half) + part * half, 32)
        attn_part[index * half : (index + 1) * half, :] = attn_weight[pl.ds(start, half), :]
    step = 256

    def tile(index, carry):
        columns = pl.ds(pl.multiple_of(index * step, step), step)
        acc = lax.dot_general(act[...], weight[columns, :], NT, preferred_element_type=F32)
        acc = acc + lax.dot_general(attended[...], attn_part[columns, :], NT, preferred_element_type=F32)
        out[:, columns] = acc.astype(BF16)
        return carry

    lax.fori_loop(0, row // step, tile, 0)


def output_part(chunk, ids, act, attended, attn_weight, pieces):
    rows, units = act.shape
    columns = sum(piece.shape[0] for piece in pieces)
    return pl.pallas_call(
        functools.partial(output_kernel, chunk),
        out_shape=jax.ShapeDtypeStruct((rows, columns), BF16),
        in_specs=[SMEM] + [VMEM] * (3 + len(pieces)),
        out_specs=VMEM,
        scratch_shapes=[pltpu.VMEM((columns, units), BF16), pltpu.VMEM((columns, attended.shape[1]), BF16)],
        compiler_params=pltpu.CompilerParams(vmem_limit_bytes=24 * MIB),
        cost_estimate=cost(2 * rows * columns * (units + attended.shape[1]), 8 * MIB),
    )(ids, act, attended, attn_weight, *pieces)


def split_three(first, second, third):
    lane = lax.broadcasted_iota(jnp.int32, first.shape, 1)
    return (
        first,
        jnp.where(lane < 32, pltpu.roll(first, 32, 1), pltpu.roll(second, 32, 1)),
        jnp.where(lane < 64, pltpu.roll(second, 64, 1), pltpu.roll(third, 64, 1)),
        pltpu.roll(third, 96, 1),
    )


def join_four(one, two, three, four):
    lane = lax.broadcasted_iota(jnp.int32, one.shape, 1)
    two, three, four = pltpu.roll(two, 96, 1), pltpu.roll(three, 64, 1), pltpu.roll(four, 32, 1)
    return jnp.concatenate(
        [jnp.where(lane < 96, one, two), jnp.where(lane < 64, two, three), jnp.where(lane < 32, three, four)], axis=1
    )


def finish_kernel(
    chunks, ids, request_group, step_index, counts, slot_of, text, image, extra, mod_table, final_table, proj, *refs
):
    sums, (text_out, image_out, extra_out, velocity, hidden, parts) = refs[: 3 * chunks], refs[3 * chunks :]
    here, there = steps_of(ids, request_group, step_index)
    count = counts[ids[0] * 8 + ids[1]]
    z, y = ids[0] // 4, ids[0] % 4
    rows_text, rows_image = text.shape[0], image.shape[0]
    filled = 0
    for chunk in range(chunks):
        own, one, two = sums[3 * chunk : 3 * chunk + 3]
        total = own[...] + one[...].astype(F32) + two[...].astype(F32)
        for half in range(total.shape[1] // 384):
            tiles = [total[:, (3 * half + i) * 128 : (3 * half + i + 1) * 128] for i in range(3)]
            for index, part in enumerate(split_three(*tiles)):
                parts[filled + 4 * half + index] = part
        filled += 4 * (total.shape[1] // 384)
    width = 384
    for pair in range(8):
        found = []
        for group in (2 * pair, 2 * pair + 1):
            dz = lax.rem(group // 4 - z + 4, 4)
            dy = lax.rem(group % 4 - y + 4, 4)
            found += [parts[slot_of[part * 16 + dz * 4 + dy]] for part in range(2)]
        total = join_four(*found)
        columns = slice(pair * width, (pair + 1) * width)
        gate = mod_table[here, 2:3, columns]
        text_out[:, columns] = (text[:, columns].astype(F32) + gate * total[:rows_text]).astype(BF16)
        states = image[:, columns].astype(F32) + gate * total[rows_text : rows_text + rows_image]
        hidden[:, columns] = states
        image_out[:, columns] = states.astype(BF16)
        gate = mod_table[there, 2:3, columns]
        slots = extra[:, columns].astype(F32) + gate * total[rows_text + rows_image :]
        live = lax.broadcasted_iota(jnp.int32, slots.shape, 0) < count
        extra_out[:, columns] = jnp.where(live, slots, 0.0).astype(BF16)
    shift, scale = final_table[here, 0:1, :], final_table[here, 1:2, :]
    normed = (layer_norm(hidden[...]) * (1.0 + scale) + shift).astype(BF16)
    velocity[...] = lax.dot_general(normed, proj[...], NT, preferred_element_type=F32)


def finish(scalars, text, image, extra, mod_table, final_table, proj, sums):
    width = text.shape[1]
    flat = [part for chunk in sums for part in chunk]
    slot_of = [0] * 32
    for index, (part, dz, dy) in enumerate(place for chunk in LAYOUT for place in chunk):
        slot_of[part * 16 + (dz % 4) * 4 + dy % 4] = index
    rows = flat[0].shape[0]
    return pl.pallas_call(
        functools.partial(finish_kernel, len(sums)),
        out_shape=(
            jax.ShapeDtypeStruct(text.shape, BF16),
            jax.ShapeDtypeStruct(image.shape, BF16),
            jax.ShapeDtypeStruct(extra.shape, BF16),
            jax.ShapeDtypeStruct((image.shape[0], proj.shape[0]), F32),
        ),
        in_specs=[SMEM] * 5 + [VMEM] * (6 + len(flat)),
        out_specs=(VMEM,) * 4,
        scratch_shapes=[pltpu.VMEM((image.shape[0], width), F32), pltpu.VMEM((32, rows, 128), F32)],
        compiler_params=pltpu.CompilerParams(vmem_limit_bytes=20 * MIB),
        cost_estimate=cost(1e7, 5 * MIB),
    )(*scalars, jnp.array(slot_of, jnp.int32), text, image, extra, mod_table, final_table, proj, *flat)


def smooth_kernel(columns, delta, above, middle, below, stencil, latent, out):
    rows = middle.shape[0]
    cells = jnp.concatenate([above[...], middle[...], below[...]], axis=0)
    column = lax.rem(lax.broadcasted_iota(jnp.int32, middle.shape, 0), columns)
    total = jnp.zeros(middle.shape, F32)
    for row_tap in range(3):
        band = cells[row_tap * columns : row_tap * columns + rows]
        for col_tap in range(3):
            moved = band if col_tap == 1 else pltpu.roll(band, (1 - col_tap) % rows, 0)
            place = column + (col_tap - 1)
            moved = jnp.where((place >= 0) & (place < columns), moved, 0.0)
            tap = 3 * row_tap + col_tap
            total = total + stencil[tap : tap + 1, :] * moved
    out[...] = latent[...] + delta[0] * total


def smooth(delta, above, middle, below, stencil, latent, columns):
    return pl.pallas_call(
        functools.partial(smooth_kernel, columns),
        out_shape=jax.ShapeDtypeStruct(middle.shape, F32),
        in_specs=[SMEM] + [VMEM] * 5,
        out_specs=VMEM,
        cost_estimate=cost(1e5, 1e5),
    )(delta, above, middle, below, stencil, latent)


def rope_tables(positions, head_dim):
    angle_list, signs = [], []
    for axis_id, section in enumerate(section_widths(head_dim)):
        half_width = section // 2
        exponent = -2.0 * jnp.arange(half_width, dtype=F32) / section
        frequency = jnp.power(F32(ROPE_BASE), exponent)
        angles = positions[axis_id].astype(F32)[:, None] * frequency[None, :]
        angle_list += [angles, angles]
        signs += [-1.0] * half_width + [1.0] * half_width
    angles = jnp.concatenate(angle_list, axis=1)
    return jnp.cos(angles), jnp.sin(angles) * jnp.array(signs, F32)[None, :]


def noise_level(step_value):
    level = 1.0 - step_value.astype(F32) / STEPS
    return 3.0 * level / (1.0 + 2.0 * level)


def per_device(
    text_tokens,
    image_tokens,
    extra_tokens,
    text_pos,
    image_pos,
    extra_pos,
    extra_counts,
    request_group,
    step_index,
    mod_table,
    final_table,
    qkv_weight,
    q_scale,
    k_scale,
    attn_out_weight,
    mlp_in_weight,
    mlp_out_weight,
    proj_weight,
    stencil,
    latent,
):
    group = lax.axis_index("wide")
    member = lax.axis_index("narrow")
    z, y = group // 4, group % 4
    chip, core = member // 2, member % 2
    ids = jnp.stack([group, member]).astype(jnp.int32)
    scalars = (ids, request_group, step_index)
    text_own, image_own, extra_own = text_tokens[0], image_tokens[0], extra_tokens[0]

    channels = proj_weight.shape[1]
    latent_rows = latent[0].reshape(-1, channels)
    hidden_weight = lax.all_gather(mlp_in_weight, "wide", axis=0, tiled=True)
    own = modulate(scalars, text_own, image_own, extra_own, mod_table)

    together = lax.optimization_barrier
    out_weight = mlp_out_weight.T
    size = out_weight.shape[0] // 2
    routes = ((along_y, along_z), (along_z, along_y))
    mine = [out_weight[:size], out_weight[size:]]
    near = [wide(mine[i], routes[i][0](step)) for i in range(2) for step in (1, -1)]
    *near, own = together((*near, own))

    def swap(block):
        return lax.ppermute(block, "narrow", CORE_SWAP)

    nxt = lax.ppermute(own, "narrow", chip_shift(-1))
    prv = lax.ppermute(own, "narrow", chip_shift(1))
    own_swapped = swap(own)
    far = [wide(near[2 * i], routes[i][0](1)) for i in range(2)]
    *far, nxt, prv, own_swapped, attn_weight, late_latent = together(
        (*far, nxt, prv, own_swapped, attn_out_weight.T, latent_rows)
    )

    cut = own.shape[0] // 2
    far_a = lax.ppermute(nxt[:cut], "narrow", chip_shift(-1))
    far_b = lax.ppermute(prv[cut:], "narrow", chip_shift(1))
    near_swapped = swap(jnp.concatenate([nxt, prv], axis=0))
    low = [jnp.concatenate([mine[i], near[2 * i]], axis=0) for i in range(2)]
    high = [jnp.concatenate([near[2 * i + 1], far[i]], axis=0) for i in range(2)]
    early = [wide(low[0], routes[0][1](1)), wide(high[0], routes[0][1](-1))]
    far_a, far_b, near_swapped, low[1], high[1] = together((far_a, far_b, near_swapped, low[1], high[1]))
    across = jnp.concatenate([far_a, far_b], axis=0)
    early += [wide(low[1], routes[1][1](1)), wide(high[1], routes[1][1](-1))]
    rows = own.shape[0]
    x = jnp.concatenate(
        [own, nxt, across, prv, own_swapped, near_swapped[:rows], swap(across), near_swapped[rows:]], axis=0
    )

    block_ids = jnp.arange(8, dtype=jnp.int32)
    sources = ((chip + block_ids % 4) % 4) * 2 + (core ^ (block_ids // 4))

    def by_block(array):
        chosen = (sources[:, None] == block_ids[None, :])[None, :, :, None]
        return jnp.sum(jnp.where(chosen, array[:, 0].reshape(3, 1, 8, -1), 0), axis=2)

    positions = jnp.concatenate([by_block(text_pos), by_block(image_pos), by_block(extra_pos)], axis=2)
    cosine, sine = rope_tables(positions.reshape(3, -1), 128)
    request_heads, extra_heads = project_heads(
        x, qkv_weight, jnp.stack([q_scale, k_scale]), cosine, sine, 8, extra_own.shape[0]
    )

    heads, slots = extra_heads.shape[1], extra_heads.shape[2]
    extra_heads, *early = together((extra_heads, *early))
    shared = extra_heads[1:].reshape(1, 2 * heads, slots, 128)
    before, after = wide(shared, along_y(1)), wide(shared, along_y(-1))

    def rest(i):
        ahead = jnp.concatenate([high[i], early[2 * i]], axis=0)
        back = jnp.concatenate([low[i], early[2 * i + 1]], axis=0)
        return ahead, back

    ahead, back = rest(1)
    before, after, ahead, back = together((before, after, ahead, back))
    first, second = wide(before[:, :heads], along_y(1)), wide(after[:, heads:], along_y(-1))
    late = [[wide(ahead, routes[1][1](1)), wide(back, routes[1][1](-1))]]
    attended = attend_request(request_heads)
    key_quad = jnp.concatenate([shared, before, after, jnp.concatenate([first, second], axis=1)], axis=0)
    above, below = wide(key_quad, along_z(1)), wide(key_quad, along_z(-1))
    ahead, back = rest(0)
    above, below, ahead, back, x, attended = together((above, below, ahead, back, x, attended))
    first, second = wide(above[:2], along_z(1)), wide(below[2:], along_z(-1))
    late.append([wide(ahead, routes[0][1](1)), wide(back, routes[0][1](-1))])
    act = hidden_units(x, hidden_weight)
    act, first, second = together((act, first, second))
    key_pieces = (key_quad, above, below, first, second)
    order = jnp.array(RING_ORDER, jnp.int32)
    groups = ((z + order) % 4)[:, None] * 4 + ((y + order) % 4)[None, :]
    owners = groups.reshape(16, 1) * 8 + sources[None, :]
    device_ids = jnp.arange(extra_counts.shape[0], dtype=jnp.int32)
    chosen = owners.reshape(-1)[:, None] == device_ids[None, :]
    counts = jnp.sum(jnp.where(chosen, extra_counts[None, :], 0), axis=1)
    slot_ids = jnp.arange(extra_own.shape[0], dtype=jnp.int32)
    live = (slot_ids[None, :] < counts[:, None]).astype(F32).reshape(1, -1)
    attended = attend_extra(extra_heads, live, attended, key_pieces, 8)

    chunks = [low[:1] + high[:1] + low[1:] + high[1:] + early] + late

    def output(i, act):
        return output_part(i, ids, act, attended, attn_weight, chunks[i])

    part0 = output(1, act)
    other0 = to_core(part0)
    part1 = output(2, act)
    other0, part1, act = together((other0, part1, act))
    far0 = to_far(part0, other0)
    other1 = to_core(part1)
    part2 = output(0, act)
    *far0, other1, part2 = together((*far0, other1, part2))
    sum0 = to_near(*far0)
    far1 = to_far(part1, other1)
    other2 = to_core(part2)
    *far1, other2 = together((*far1, other2))
    sum1 = to_near(*far1)
    far2 = to_far(part2, other2)
    sums = [to_near(*far2), sum0, sum1]
    text_out, image_out, extra_out, velocity = finish(
        (*scalars, extra_counts), text_own, image_own, extra_own, mod_table, final_table, proj_weight.T, sums
    )
    grid_width = latent.shape[2] // channels
    above = lax.ppermute(velocity[-grid_width:], "narrow", [(i, i + 1) for i in range(7)])
    below = lax.ppermute(velocity[:grid_width], "narrow", [(i + 1, i) for i in range(7)])
    step_here = step_index[request_group[group]]
    delta = (noise_level(step_here + 1) - noise_level(step_here)).reshape(1)
    latent_next = smooth(
        delta, above, velocity, below, stencil, late_latent, grid_width
    )
    return (text_out[None], image_out[None], extra_out[None], latent_next.reshape(latent.shape))


def solution(mesh):
    return jax.shard_map(
        per_device,
        mesh=mesh,
        in_specs=(
            P("wide", "narrow", None),
            P("wide", "narrow", None),
            P("wide", "narrow", None),
            P(None, "wide", None),
            P(None, "wide", None),
            P(None, "wide", None),
            P(),
            P(),
            P(),
            P(),
            P(),
            P(None, None, "narrow"),
            P(),
            P(),
            P("narrow", None),
            P("wide", "narrow"),
            P("narrow", "wide"),
            P(),
            P(),
            P("wide", "narrow", None),
        ),
        out_specs=(
            P("wide", "narrow", None),
            P("wide", "narrow", None),
            P("wide", "narrow", None),
            P("wide", "narrow", None),
        ),
        check_vma=False,
    )
```
